128 devices in a mesh: rep: 4 (over y), exp: 8 (over x, core), seq: 4 (over z).
Axes of the slice: x: 4, y: 4, z: 4, core: 2. Of those that a mesh axis runs over, the one named last changes fastest.
Arguments:
- tokens: bfloat16 [16384, 1024], P(('rep', 'exp', 'seq')), may hold values from -6 to 6
- norm1_gain: bfloat16 [1024], P(('rep', 'exp', 'seq')), may hold values from 0.5 to 1.5
- w_query: bfloat16 [1024, 1024], P(('rep', 'exp', 'seq')), may hold values from -0.25 to 0.25
- w_keyval: bfloat16 [1024, 1024], P(('rep', 'exp', 'seq')), may hold values from -0.25 to 0.25
- w_output: bfloat16 [1024, 1024], P(('rep', 'exp', 'seq')), may hold values from -0.75 to 0.75
- norm2_gain: bfloat16 [1024], P(('rep', 'exp', 'seq')), may hold values from 0.5 to 1.5
- w_router: bfloat16 [1024, 32], P(('rep', 'exp', 'seq')), may hold values from -0.09375 to 0.09375
- expert_in: bfloat16 [32, 1024, 1024], P('exp'), may hold values from -0.1875 to 0.1875
- expert_out: bfloat16 [32, 512, 1024], P('exp'), may hold values from -0.5 to 0.5
- routes: int32 [16384, 8], P(('rep', 'exp', 'seq')), may hold values from 0 to 31, all different within a row; in each aligned block of 128 rows (0 to 127, 128 to 255, ...) at most 64 rows name the same one
- cotangent: bfloat16 [16384, 1024], P(('rep', 'exp', 'seq')), may hold values from -6 to 6
Outputs:
- output: bfloat16 [16384, 1024], P(('rep', 'exp', 'seq'))
- grad_tokens: float32 [16384, 1024], P(('rep', 'exp', 'seq'))
- grad_norm1: float32 [1024], P(('rep', 'exp', 'seq'))
- grad_query: float32 [1024, 1024], P(('rep', 'exp', 'seq'))
- grad_keyval: float32 [1024, 1024], P(('rep', 'exp', 'seq'))
- grad_output: float32 [1024, 1024], P(('rep', 'exp', 'seq'))
- grad_norm2: float32 [1024], P(('rep', 'exp', 'seq'))
- grad_router: float32 [1024, 32], P(('rep', 'exp', 'seq'))
- grad_expert_in: float32 [32, 1024, 1024], P('exp', ('rep', 'seq'))
- grad_expert_out: float32 [32, 512, 1024], P('exp', ('rep', 'seq'))
The draws below stay inside these ranges and needn't reach their ends.
Inputs may be any that keep to these rules, and one draw needn't show every extreme that they name: `routes`: in the rows of one device (aligned blocks of 128 rows) no expert is named by more than 64 rows, a bound that some block reaches.
All inputs are finite; a program needn't handle non-finite values.
Results may differ from the reference program's by a relative error of at most 0.04.
Values may be sent and summed in bfloat16 or wider, within the bound.
No kernel may reach another device: no remote copies, remote signals or barrier semaphores. Data moves between devices by JAX's collectives and lax.ppermute only.
A program may use at most 192 MiB of HBM per device.

```python
import math
import jax
import jax.numpy as jnp
import numpy as np
from jax import lax

D = 1024
H = 16
KV = 8
HD = 64
F = 512
TOP = 8
TOK_DEV = 128
EXPERTS = 32
SEQ_LEN = 4096
TOKENS = 16384
CAP = 64
N_REP = 4
N_EXP = 8
N_SEQ = 4


def block_scale(stream_key, dims, pieces, smallest, high):
    def one(dim, blocks):
        heights = jax.random.uniform(jax.random.fold_in(jax.random.fold_in(stream_key, 6), dim), (blocks,), jnp.float32, smallest / len(pieces), high / len(pieces))
        return jnp.repeat(jnp.exp(heights), dims[dim] // blocks).reshape((-1,) + (1,) * (len(dims) - dim - 1))

    loudness = one(*pieces[0])
    for cut in pieces[1:]:
        loudness = loudness * one(*cut)
    return loudness


def routed_block(key, own, number, rows, count, top, most, lean):
    sequence = jax.random.permutation(key, count)
    packed, common = load_shares(count, rows * top, most, lean, True), load_shares(count, rows * top, most, lean, False)
    places = jnp.arange(count)

    def named(sizes, rotation):
        used = int((sizes > 0).sum())
        fixed = max(1, used // 4)
        shifted = fixed + (places - fixed + rotation * (used - fixed)) % max(1, count - fixed)
        return jnp.zeros((count,), jnp.int32).at[sequence[jnp.where(places < fixed, places, shifted)]].set(jnp.asarray(sizes, jnp.int32))

    sizes = jnp.where(number % 4 == 0, named(packed, number // 4), named(common, number - number // 4 - 1))
    mixed = jax.random.permutation(jax.random.fold_in(own, 3), count)
    source_of, sink = mixed[0:count // 2 * 2:2], mixed[1:count // 2 * 2:2]
    margin = jnp.minimum(sizes[source_of] - 1, most - sizes[sink]) // 2
    margin = jnp.where((source_of == sequence[0]) | (sink == sequence[0]) | (sizes[sink] == 0), 0, jnp.maximum(margin, 0))
    shifted = jax.random.randint(jax.random.fold_in(own, 4), (count // 2,), 0, 1 << 20) % (margin + 1)
    sizes = sizes.at[source_of].add(-shifted).at[sink].add(shifted)
    members = jnp.searchsorted(jnp.cumsum(sizes), jnp.arange(rows * top), side="right").astype(jnp.int32)
    listing = members.reshape(top, rows).T
    listing = listing[jax.random.permutation(jax.random.fold_in(own, 1), rows)]
    rotation = jax.random.randint(jax.random.fold_in(own, 2), (rows, 1), 0, top)
    return jnp.take_along_axis(listing, (jnp.arange(top)[None, :] + rotation) % top, axis=1)


def load_shares(number_of, total, bound, slope, full):
    weights = [(1 << 20) // math.isqrt(grade ** slope) + 1 for grade in range(1, number_of + 1)]
    largest = bound if full else min(bound, max(-(-total // number_of), total * weights[0] // sum(weights)))
    least = 1 if total - largest >= number_of - 1 else 0
    counts, rest = [largest] + [least] * (number_of - 1), total - largest - least * (number_of - 1)
    while rest > 0:
        free = [i for i in range(1, number_of) if counts[i] < largest] or [i for i in range(1, number_of) if counts[i] < bound]
        mass, left = sum([weights[i] for i in free]), rest
        for i in free:
            addition = min(bound - counts[i], max(1, left * weights[i] // mass), rest)
            counts[i] = counts[i] + addition
            rest = rest - addition
    return np.array(counts)


def centred(own_key, shape, spread, most, pieces=(), kind=jnp.bfloat16):
    values = jax.random.normal(own_key, shape, jnp.float32) * spread
    if len(pieces) > 0:
        values = block_scale(own_key, shape, pieces, -0.22, 0.18) * values
    return jnp.clip(values, min=-most, max=most).astype(kind)


def setup_inputs(seed: int = 0) -> dict:
    key_of = jax.random.split(jax.random.key(seed), 12)
    tokens = centred(key_of[0], (TOKENS, D), 1.0, 6.0, ((0, 128),))
    norm1_gain = jnp.clip(1.0 + 0.1 * jax.random.normal(key_of[1], (D,), jnp.float32), 0.5, 1.5).astype(jnp.bfloat16)
    w_query = centred(key_of[2], (D, H * HD), (D // 2) ** -0.5, 0.25, ((0, 128),))
    w_keyval = centred(key_of[3], (D, 2 * KV * HD), (D // 2) ** -0.5, 0.25, ((0, 128),))
    w_output = centred(key_of[4], (H * HD, D), (H * HD // 16) ** -0.5, 0.75, ((0, 128),))
    norm2_gain = jnp.clip(1.0 + 0.1 * jax.random.normal(key_of[5], (D,), jnp.float32), 0.5, 1.5).astype(jnp.bfloat16)
    w_router = centred(key_of[6], (D, EXPERTS), (4 * D) ** -0.5, 0.09375, ((0, 128),))
    expert_in = centred(key_of[7], (EXPERTS, D, 2 * F), D ** -0.5, 0.1875, ((0, 8),))
    expert_out = centred(key_of[8], (EXPERTS, F, D), (F // 4) ** -0.5, 0.5, ((0, 8),))
    routes_keys = jax.random.split(jax.random.fold_in(key_of[9], 1), TOKENS // TOK_DEV)
    routes_turns = jax.random.permutation(jax.random.fold_in(key_of[9], 3), TOKENS // TOK_DEV)
    routes = jax.vmap(lambda own, number: routed_block(jax.random.fold_in(key_of[9], 2), own, number, TOK_DEV, EXPERTS, TOP, CAP, 2))(routes_keys, routes_turns).reshape((TOKENS, TOP))
    cotangent = centred(key_of[10], (TOKENS, D), 1.0, 6.0, ((0, 128),))
    return dict(tokens=tokens, norm1_gain=norm1_gain, w_query=w_query, w_keyval=w_keyval, w_output=w_output, norm2_gain=norm2_gain, w_router=w_router, expert_in=expert_in, expert_out=expert_out, routes=routes, cotangent=cotangent)


@jax.custom_vjp
def low(v):
    return lax.optimization_barrier(v.astype(jnp.bfloat16)).astype(jnp.float32)

@jax.custom_vjp
def low_back(v):
    return v

def low_keep(v):
    return (low(v), None)

def low_pass(kept, grad):
    return (grad,)

def back_keep(v):
    return (v, None)

def back_low(kept, grad):
    return (low(grad),)
low.defvjp(low_keep, low_pass)
low_back.defvjp(back_keep, back_low)
highest = lax.Precision.HIGHEST
epsilon = 1e-06

def rotate(vectors, positions):
    half_size = vectors.shape[-1] // 2
    frequencies = 10000.0 ** (-(jnp.arange(half_size, dtype=jnp.float32) * 2.0 / vectors.shape[-1]))
    angles = positions.astype(jnp.float32)[:, None] * frequencies[None, :]
    cosine = jnp.cos(angles)[:, None, :]
    sine_table = jnp.sin(angles)[:, None, :]
    leading = vectors[..., :half_size]
    trailing = vectors[..., half_size:]
    return jnp.concatenate([leading * cosine - trailing * sine_table, trailing * cosine + leading * sine_table], axis=-1)

def rms_scale(vectors, gain_vector):
    mean_square = lax.optimization_barrier(jnp.mean(vectors * vectors, axis=-1, keepdims=True))
    return vectors * lax.rsqrt(mean_square + epsilon) * gain_vector

def attend_sequence(triple):
    queries, key_rows, value_rows = triple
    length = queries.shape[0]
    block_rows = min(512, length)
    groups = H // KV
    score_scale = HD ** (-0.5)
    query_blocks = queries.reshape(length // block_rows, block_rows, KV, groups, HD)
    starts = jnp.arange(length // block_rows, dtype=jnp.int32) * block_rows
    key_positions = jnp.arange(length, dtype=jnp.int32)

    def one_block(pair):
        query_block, offset = pair
        scores = jnp.einsum('tkgd,nkd->kgtn', query_block, key_rows, precision=highest) * score_scale
        scores = low_back(scores)
        query_positions = offset + jnp.arange(block_rows, dtype=jnp.int32)
        allowed = query_positions[:, None] >= key_positions[None, :]
        scores = jnp.where(allowed, scores, -1e+30)
        weights = low(jax.nn.softmax(scores, axis=-1))
        attended = jnp.einsum('kgtn,nkd->tkgd', weights, value_rows, precision=highest)
        return attended.reshape(block_rows, H * HD)
    return lax.map(jax.checkpoint(one_block), (query_blocks, starts)).reshape(length, H * HD)

def expert_apply(rows, weight_in, weight_out):
    projected = low_back(jnp.dot(rows, weight_in, precision=highest))
    active = low(jax.nn.silu(projected[:, :F]) * projected[:, F:])
    return low(low_back(jnp.dot(active, weight_out, precision=highest)))

def reference(tokens, norm1_gain, w_query, w_keyval, w_output, norm2_gain, w_router, expert_in, expert_out, routes, cotangent):
    devices_all = N_REP * N_EXP * N_SEQ
    route_count = TOK_DEV * TOP
    blocks = routes.reshape(devices_all, route_count)
    one_hot = (blocks[:, :, None] == jnp.arange(EXPERTS, dtype=jnp.int32)[None, None, :]).astype(jnp.int32)
    slot_ranks = lax.optimization_barrier(jnp.sum(jnp.cumsum(one_hot, axis=1) * one_hot, axis=2)) - 1
    slot_index = blocks * CAP + slot_ranks
    device_ids = jnp.broadcast_to(jnp.arange(devices_all, dtype=jnp.int32)[:, None], (devices_all, route_count))
    route_ids = device_ids * route_count + jnp.arange(route_count, dtype=jnp.int32)[None, :]
    slot_table = jnp.full((devices_all, EXPERTS * CAP), TOKENS * TOP, jnp.int32).at[device_ids, slot_index].set(route_ids)
    slot_routes = slot_table.reshape(devices_all, EXPERTS, CAP).transpose(1, 0, 2).reshape(EXPERTS, devices_all * CAP)
    slot_tokens = slot_routes // TOP
    positions = jnp.tile(jnp.arange(SEQ_LEN, dtype=jnp.int32), N_REP)

    def forward(token_f, gain_one, query_w, keyval_w, output_w, gain_two, router_w, weight_in, weight_out):
        hidden1 = low(rms_scale(token_f, gain_one))
        query_raw = low_back(jnp.dot(hidden1, query_w, precision=highest))
        keyval_raw = low_back(jnp.dot(hidden1, keyval_w, precision=highest))
        queries = low(rotate(query_raw.reshape(TOKENS, H, HD), positions))
        key_rows = low(rotate(keyval_raw[:, :KV * HD].reshape(TOKENS, KV, HD), positions))
        value_rows = low(keyval_raw[:, KV * HD:].reshape(TOKENS, KV, HD))
        attended = lax.map(attend_sequence, (queries.reshape(N_REP, SEQ_LEN, H, HD), key_rows.reshape(N_REP, SEQ_LEN, KV, HD), value_rows.reshape(N_REP, SEQ_LEN, KV, HD)))
        attended = low(low_back(attended.reshape(TOKENS, H * HD)))
        branch = low_back(jnp.dot(attended, output_w, precision=highest))
        middle = token_f + branch
        hidden2 = low(rms_scale(middle, gain_two))
        logits = low_back(jnp.dot(hidden2, router_w, precision=highest))
        chosen = jnp.take_along_axis(logits, routes, axis=1)
        gate_weights = jax.nn.softmax(chosen, axis=-1)
        extended = jnp.concatenate([hidden2, jnp.zeros((1, D), hidden2.dtype)], axis=0)

        def per_expert(triple):
            token_ids, one_in, one_out = triple
            rows = low_back(extended[token_ids])
            return expert_apply(rows, one_in, one_out)
        produced = lax.map(jax.checkpoint(per_expert), (slot_tokens, weight_in, weight_out))
        combined = jnp.zeros((TOKENS * TOP + 1, D), hidden2.dtype).at[slot_routes.reshape(-1)].add(produced.reshape(-1, D))
        per_route = combined[:TOKENS * TOP].reshape(TOKENS, TOP, D)
        mixture = lax.optimization_barrier(jnp.sum(gate_weights[:, :, None] * per_route, axis=1))
        return middle + mixture
    inputs = (tokens.astype(jnp.float32), norm1_gain.astype(jnp.float32), w_query.astype(jnp.float32), w_keyval.astype(jnp.float32), w_output.astype(jnp.float32), norm2_gain.astype(jnp.float32), w_router.astype(jnp.float32), expert_in.astype(jnp.float32), expert_out.astype(jnp.float32))
    result, pullback = jax.vjp(forward, *inputs)
    grads = pullback(cotangent.astype(jnp.float32))
    return (result.astype(jnp.bfloat16), grads[0], grads[1], grads[2], grads[3], grads[4], grads[5], grads[6], grads[7], grads[8])
```

```python
import functools

import jax
import jax.numpy as jnp
from jax import lax
from jax.experimental import pallas as pl
from jax.experimental.pallas import tpu as pltpu
from jax.sharding import PartitionSpec as P

H = 16
KV = 8
HD = 64
F = 512
TOP = 8
CAP = 64

epsilon = 1e-06
f32 = jnp.float32
bf16 = jnp.bfloat16

VMEM = pl.BlockSpec(memory_space=pltpu.VMEM)
SMEM = pl.BlockSpec(memory_space=pltpu.SMEM)


def dot(a, b):
    return jnp.dot(a, b, preferred_element_type=f32)


def dot_t(a, b):
    return lax.dot_general(a, b, (((1,), (1,)), ((), ())), preferred_element_type=f32)


def t_dot(a, b):
    return lax.dot_general(a, b, (((0,), (0,)), ((), ())), preferred_element_type=f32)


def call(body, out_shape, flops, nbytes, **kw):
    return pl.pallas_call(
        body,
        out_shape=out_shape,
        cost_estimate=pl.CostEstimate(flops=flops, bytes_accessed=nbytes, transcendentals=0),
        compiler_params=pltpu.CompilerParams(vmem_limit_bytes=60 * 1024 * 1024),
        **kw,
    )


def whole(body, out_shape, n_in, flops, nbytes, scalars=0, scratch=()):
    outs = jax.tree.map(lambda _: VMEM, out_shape)
    return call(
        body,
        out_shape,
        flops,
        nbytes,
        in_specs=[SMEM] * scalars + [VMEM] * (n_in - scalars),
        out_specs=outs,
        scratch_shapes=list(scratch),
    )


def shape(dims, dtype):
    return jax.ShapeDtypeStruct(dims, dtype)


def turn(vectors, cosine, sine):
    half = vectors.shape[0] // 2
    a, b = vectors[:half], vectors[half:]
    return jnp.concatenate([a * cosine - b * sine, b * cosine + a * sine], axis=0)


def lanes(rows):
    return lax.broadcasted_iota(jnp.int32, (rows, 128), 1)


def pack_kernel(
    q_ref, kv_ref, gain_ref, routes_ref, out_w_ref, router_ref, gain_two_ref, out_ref, rest_ref
):
    n, rows, _ = out_ref.shape
    width = out_w_ref.shape[1]
    experts = router_ref.shape[1]
    low = lanes(rows) < HD
    same = lax.broadcasted_iota(jnp.int32, (rows, rows), 0) == lax.broadcasted_iota(
        jnp.int32, (rows, rows), 1
    )

    def column(ref):
        return jnp.sum(jnp.where(same, ref[...].astype(f32), 0.0), axis=1, keepdims=True)

    gain = column(gain_ref)
    routes = routes_ref[...].astype(f32).astype(bf16)
    for e in range(n):
        at = e // 2 * 128
        key = kv_ref[:, at : at + 128].astype(f32)
        value = kv_ref[:, KV * HD + at : KV * HD + at + 128].astype(f32)
        if e % 2 == 0:
            pair = jnp.where(low, key, pltpu.roll(value, HD, 1))
        else:
            pair = jnp.where(low, pltpu.roll(key, HD, 1), value)
        query = q_ref[:, e * 2 * HD : (e + 1) * 2 * HD].astype(f32)
        out_ref[e] = jnp.concatenate(
            [(gain * query).astype(bf16), (gain * pair).astype(bf16), routes], axis=1
        )
    router = jnp.concatenate(
        [router_ref[...].astype(f32), jnp.zeros((rows, 128 - experts), f32)], axis=1
    )
    router = jnp.where(lanes(rows) == experts, column(gain_two_ref), router)
    rest_ref[...] = jnp.concatenate([out_w_ref[...], router.astype(bf16)], axis=1)


def pack_call(w_query, w_keyval, gain, routes, w_output, w_router, gain_two, n_exp):
    rows, width = w_output.shape
    return whole(
        pack_kernel,
        [shape((n_exp, rows, 4 * HD + 128), bf16), shape((rows, width + 128), bf16)],
        7,
        1000,
        n_exp * rows * 768,
    )(w_query, w_keyval, gain, routes, w_output, w_router, gain_two)


def group_sums(got_ref, n_exp, n_seq):
    n_all = got_ref.shape[0]
    total = []
    for e in range(n_exp):
        one = jnp.zeros(got_ref.shape[1:], f32)
        for r in range(n_all // (n_exp * n_seq)):
            for z in range(n_seq):
                one = one + got_ref[(r * n_exp + e) * n_seq + z].astype(f32)
        total.append(one)
    return total


def unpack_kernel(
    n_exp,
    n_seq,
    got_ref,
    wq_ref,
    wkv_ref,
    gain_ref,
    q_ref,
    kv_ref,
    out_ref,
    router_ref,
    gain_one_ref,
    gain_two_ref,
):
    total = group_sums(got_ref, n_exp, n_seq)
    rows = q_ref.shape[0]
    low = lanes(rows) < HD
    same = lax.broadcasted_iota(jnp.int32, (rows, rows), 0) == lax.broadcasted_iota(
        jnp.int32, (rows, rows), 1
    )
    gain = jnp.sum(jnp.where(same, gain_ref[...].astype(f32), 0.0), axis=1, keepdims=True)
    part = jnp.zeros((rows, 128), f32)
    for e in range(n_exp):
        at = slice(e * 2 * HD, (e + 1) * 2 * HD)
        part = part + wq_ref[:, at].astype(f32) * total[e][:, : 2 * HD]
        q_ref[:, at] = gain * total[e][:, : 2 * HD]
        out_ref[:, at] = total[e][:, 2 * HD : 4 * HD]
    for e in range(0, n_exp, 2):
        a = total[e][:, 4 * HD + 128 :]
        b = total[e + 1][:, 4 * HD + 128 :]
        at = e // 2 * 128
        for at, piece in (
            (at, jnp.where(low, a, pltpu.roll(b, HD, 1))),
            (at + KV * HD, jnp.where(low, pltpu.roll(a, HD, 1), b)),
        ):
            part = part + wkv_ref[:, at : at + 128].astype(f32) * piece
            kv_ref[:, at : at + 128] = gain * piece
    small = sum(one[:, 4 * HD : 4 * HD + 128] for one in total)
    experts = router_ref.shape[1]
    router_ref[...] = small[:, :experts]
    small = jnp.where(
        lanes(rows) == experts, jnp.sum(part, axis=1, keepdims=True), small
    )
    small = jnp.concatenate([small, jnp.zeros((128 - rows, 128), f32)], axis=0).T
    gain_one_ref[...] = small[experts : experts + 1, :rows]
    gain_two_ref[...] = small[experts + 1 : experts + 2, :rows]


def unpack_call(got, w_query, w_keyval, gain, experts, n_exp, n_seq):
    n_all, rows, _ = got.shape
    wide = shape((rows, H * HD), f32)
    one = shape((1, rows), f32)
    return whole(
        functools.partial(unpack_kernel, n_exp, n_seq),
        [wide, wide, wide, shape((rows, experts), f32), one, one],
        4,
        1000,
        n_all * rows * 1024,
    )(got, w_query, w_keyval, gain)


def qkv_kernel(*refs):
    n = len(refs) - 7
    toks = refs[:n]
    w_ref, cos_ref, sin_ref, q_ref, qt_ref, kv_ref, hidden = refs[n:]
    rows = toks[0].shape[0]
    for j in range(n):
        x = toks[j][...].astype(f32)
        inverse = lax.rsqrt(jnp.mean(x * x, axis=-1, keepdims=True) + epsilon)
        hidden[j * rows : (j + 1) * rows] = (x * inverse).astype(bf16)
    whole_raw = dot(hidden[...], w_ref[...])
    for j in range(n):
        raw = whole_raw[j * rows : (j + 1) * rows]
        cosine, sine = cos_ref[j], sin_ref[j]
        up = raw[:, : 2 * HD].T
        up = jnp.concatenate(
            [turn(up[:HD], cosine, sine), turn(up[HD:], cosine, sine)], axis=0
        ) * (HD**-0.5)
        qt_ref[j] = up.astype(bf16)
        q_ref[j] = up.T.astype(bf16)
        up = raw[:, 2 * HD :].T
        up = jnp.concatenate([turn(up[:HD], cosine, sine), up[HD:]], axis=0)
        kv_ref[j] = up.T.astype(bf16)


def qkv_call(toks, w, cosine, sine):
    n = len(toks)
    rows, width = toks[0].shape
    o = shape((n, rows, 2 * HD), bf16)
    return whole(
        qkv_kernel,
        [o, o, o],
        n + 3,
        2 * n * rows * width * 4 * HD,
        4 * n * rows * width,
        scratch=[pltpu.VMEM((n * rows, width), bf16)],
    )(*toks, w, cosine, sine)


def chip_of(h, own):
    n_x = 4
    return 2 * lax.rem(h + n_x - own[0], n_x)


def fill_keys(kvs, keys, keys_up, mask, own, rows):
    n_seq, n = len(kvs), kvs[0].shape[0]
    for j in range(n):
        for d in range(n_seq):
            piece = kvs[d][j]
            keys[j, d * rows : (d + 1) * rows] = piece
            keys_up[j, :, d * rows : (d + 1) * rows] = piece.T
    query = own[2] * rows + lax.rem(
        lax.broadcasted_iota(jnp.int32, (rows, 2 * rows), 1), jnp.int32(rows)
    )
    for d in range(n_seq):
        key = lax.rem(own[2] + d, n_seq) * rows + lax.broadcasted_iota(
            jnp.int32, (rows, 2 * rows), 0
        )
        mask[d * rows : (d + 1) * rows] = jnp.where(key <= query, 0.0, -1e30).astype(f32)


def side(x):
    return jnp.concatenate([x[:HD], x[HD:]], axis=1)


def stack(x):
    rows = x.shape[1] // 2
    return jnp.concatenate([x[:, :rows], x[:, rows:]], axis=0)


def attend_kernel(own, qt_ref, *refs):
    kvs = refs[:4]
    att_ref, up_ref, log_ref, keys, keys_up, mask = refs[4:]
    n, _, rows = qt_ref.shape
    own = [own[0], own[1], own[2]]
    fill_keys(kvs, keys, keys_up, mask, own, rows)

    wide = 4 * rows

    def pair(h, _):
        at = chip_of(h, own)
        early, late = at + own[1], at + 1 - own[1]
        query = jnp.concatenate([side(qt_ref[early]), side(qt_ref[late])], axis=1)
        query = jnp.concatenate([query, jnp.zeros_like(query)], axis=0)

        def step(state, blocks):
            top, total, acc = state
            new_top = top
            for _, scores in blocks:
                new_top = jnp.maximum(new_top, jnp.max(scores, axis=0, keepdims=True))
            shrink = jnp.exp(top - new_top)
            total = total * shrink
            acc = acc * shrink
            for i, scores in blocks:
                p = jnp.exp(scores - new_top)
                total = total + jnp.sum(p, axis=0, keepdims=True)
                acc = acc + dot(keys_up[i, HD:], p.astype(bf16))
            return new_top, total, acc

        def chunk(c, state):
            i = chip_of(c, own)
            return step(state, [(i, dot(keys[i], query)), (i + 1, dot(keys[i + 1], query))])

        state = (
            jnp.full((1, wide), -1e30, f32),
            jnp.zeros((1, wide), f32),
            jnp.zeros((HD, wide), f32),
        )
        state = lax.fori_loop(0, h, chunk, state)
        scores = dot(keys[early], query)
        last = dot(keys[late], query[:, 2 * rows :])
        first = step([v[:, : 2 * rows] for v in state], [(early, scores[:, : 2 * rows] + mask[...])])
        second = step(
            [v[:, 2 * rows :] for v in state],
            [(early, scores[:, 2 * rows :]), (late, last + mask[...])],
        )
        for j, (top, total, acc) in ((early, first), (late, second)):
            up = acc / total
            up_ref[j] = up
            log_ref[j] = top + jnp.log(total)
            att_ref[j] = stack(up).T.astype(bf16)
        return 0

    lax.fori_loop(0, n // 2, pair, 0)


def attend_call(own, qt, kvs):
    n, _, rows = qt.shape
    n_seq = len(kvs)
    return whole(
        attend_kernel,
        [
            shape((n, rows, 2 * HD), bf16),
            shape((n, HD, 2 * rows), f32),
            shape((n, 1, 2 * rows), f32),
        ],
        2 + n_seq,
        36 * 4 * 512 * 256 * 128 * 2,
        4 * n * rows * 2 * HD * (n_seq + 4),
        scalars=1,
        scratch=[
            pltpu.VMEM((n, n_seq * rows, 2 * HD), bf16),
            pltpu.VMEM((n, 2 * HD, n_seq * rows), bf16),
            pltpu.VMEM((n_seq * rows, 2 * rows), f32),
        ],
    )(own, qt, *kvs)


def attend_back_kernel(own, q_ref, qt_ref, up_ref, log_ref, got_ref, cos_ref, sin_ref, *refs):
    n, _, rows = qt_ref.shape
    kvs = refs[:4]
    dq_ref = refs[4]
    dkv_refs = refs[5:9]
    keys, keys_up, mask, grads_up, dkv = refs[9:]
    own = [own[0], own[1], own[2]]
    fill_keys(kvs, keys, keys_up, mask, own, rows)
    for j in range(n):
        grads_up[j] = got_ref[j, :, : 2 * HD].T
        dkv[j] = jnp.zeros(dkv.shape[1:], f32)
    low_lane = lanes(rows) < HD
    half = 2 * rows

    def pair(h, _):
        at = chip_of(h, own)
        early, late = at + own[1], at + 1 - own[1]
        query = jnp.concatenate([side(qt_ref[early]), side(qt_ref[late])], axis=1)
        grad = jnp.concatenate([side(grads_up[2 * h]), side(grads_up[2 * h + 1])], axis=1)
        up = jnp.concatenate([up_ref[early], up_ref[late]], axis=1)
        log_total = jnp.concatenate([log_ref[early], log_ref[late]], axis=1)
        delta = jnp.sum(up * grad.astype(f32), axis=0, keepdims=True)
        query = jnp.concatenate([query, jnp.zeros_like(query)], axis=0)
        grad = jnp.concatenate([jnp.zeros_like(grad), grad], axis=0)
        below_q, below_g = [], []
        for b, j in ((2 * h, early), (2 * h + 1, late)):
            q = q_ref[j].astype(f32)
            g = got_ref[b][:, : 2 * HD].astype(f32)
            below_q.append(
                jnp.concatenate(
                    [jnp.where(low_lane, q, 0.0), jnp.where(low_lane, pltpu.roll(q, HD, 1), 0.0)],
                    axis=0,
                ).astype(bf16)
            )
            below_g.append(
                jnp.concatenate(
                    [jnp.where(low_lane, 0.0, pltpu.roll(g, HD, 1)), jnp.where(low_lane, 0.0, g)],
                    axis=0,
                ).astype(bf16)
            )
        below = jnp.concatenate(below_q + below_g, axis=0)
        below_late = jnp.concatenate([below_q[1], below_g[1]], axis=0)

        def chunk(i, acc, scores, grad_p, log_, delta_, below_):
            p = jnp.exp(scores - log_)
            ds = (p * (grad_p - delta_)).astype(bf16)
            dkv[i] = dkv[i] + dot(jnp.concatenate([ds, p.astype(bf16)], axis=1), below_)
            return acc + dot(keys_up[i, :HD], ds)

        def full(c, acc):
            i = chip_of(c, own)
            for k in (i, i + 1):
                acc = chunk(
                    k, acc, dot(keys[k], query), dot(keys[k], grad), log_total, delta, below
                )
            return acc

        acc = lax.fori_loop(0, h, full, jnp.zeros((HD, 2 * half), f32))
        scores = dot(keys[early], query)
        scores = jnp.concatenate([scores[:, :half] + mask[...], scores[:, half:]], axis=1)
        acc = chunk(early, acc, scores, dot(keys[early], grad), log_total, delta, below)
        scores = dot(keys[late], query[:, half:]) + mask[...]
        last = chunk(
            late,
            acc[:, half:],
            scores,
            dot(keys[late], grad[:, half:]),
            log_total[:, half:],
            delta[:, half:],
            below_late,
        )
        for b, j, part in ((2 * h, early, acc[:, :half]), (2 * h + 1, late, last)):
            cosine, sine = cos_ref[j], -sin_ref[j]
            cosine = jnp.concatenate([cosine, cosine], axis=1)
            sine = jnp.concatenate([sine, sine], axis=1)
            dq_ref[b] = stack(turn(part * (HD**-0.5), cosine, sine)).T.astype(bf16)
        return 0

    lax.fori_loop(0, n // 2, pair, 0)
    for d, ref in enumerate(dkv_refs):
        for j in range(n):
            ref[j] = dkv[j, d * rows : (d + 1) * rows].astype(bf16)


def attend_back_call(own, q, qt, up, log_total, got, cosine, sine, kvs):
    n, _, rows = qt.shape
    n_seq = len(kvs)
    o = shape((n, rows, 2 * HD), bf16)
    return whole(
        attend_back_kernel,
        [o] * (1 + n_seq),
        8 + n_seq,
        36 * 10 * 512 * 256 * 128 * 2,
        4 * n * rows * 2 * HD * 10,
        scalars=1,
        scratch=[
            pltpu.VMEM((n, n_seq * rows, 2 * HD), bf16),
            pltpu.VMEM((n, 2 * HD, n_seq * rows), bf16),
            pltpu.VMEM((n_seq * rows, 2 * rows), f32),
            pltpu.VMEM((n, 2 * HD, rows), bf16),
            pltpu.VMEM((n, n_seq * rows, 2 * HD), f32),
        ],
    )(own, q, qt, up, log_total, got, cosine, sine, *kvs)


def early_kernel(n, order, left_ref, dq_ref, got_ref, router_grad, gain_two_grad, *refs):
    toks = refs[:n]
    out_ref, hidden, columns = refs[n:]
    rows, width = toks[0].shape
    for j in range(n):
        own = slice(j * rows, (j + 1) * rows)
        columns[: 2 * HD, own] = dq_ref[order[j]].T
        columns[2 * HD :, own] = got_ref[order[j]][:, 2 * HD :].T
        x = toks[j][...].astype(f32)
        x = x * lax.rsqrt(jnp.mean(x * x, axis=-1, keepdims=True) + epsilon)
        hidden[own] = x.astype(bf16)
    out_ref[:, : 2 * HD] = dot(columns[: 2 * HD], hidden[...]).T.astype(bf16)
    out_ref[:, 2 * HD : 4 * HD] = dot(columns[2 * HD :], left_ref[...]).T.astype(bf16)
    gains = jnp.concatenate(
        [jnp.zeros((33, width), f32), gain_two_grad[...], jnp.zeros((94, width), f32)], axis=0
    )
    out_ref[:, 4 * HD :] = (router_grad[...] + gains.T).astype(bf16)


def early_call(order, left, dq, got, router_grad, gain_two_grad, toks):
    n = len(toks)
    rows, width = toks[0].shape
    return whole(
        functools.partial(early_kernel, n),
        [shape((width, 4 * HD + 128), bf16), shape((n * rows, width), bf16)],
        6 + n,
        4 * n * rows * width * 128,
        n * rows * width * 6,
        scalars=1,
        scratch=[pltpu.VMEM((4 * HD, n * rows), bf16)],
    )(order, left, dq, got, router_grad, gain_two_grad, *toks)


def middle_kernel(n, own, order, w_ref, routes_ref, *refs):
    att = refs[:n]
    toks = refs[n : 2 * n]
    hid_ref, mid_ref, gates_ref, rank_ref, gate_up_ref, left, gain_ref, middles = refs[2 * n :]
    rows, width = toks[0].shape
    experts = rank_ref.shape[1]
    router = w_ref[:, width:]
    gain_ref[...] = router.astype(f32).T[experts : experts + 8]
    lane = lanes(rows)
    before = (
        lax.broadcasted_iota(jnp.int32, (rows, rows), 0)
        >= lax.broadcasted_iota(jnp.int32, (rows, rows), 1)
    ).astype(bf16)
    for k in range(n):
        column = pl.ds(pl.multiple_of(order[k] * 128, 128), 128)
        for j in range(n):
            source = 2 * ((j // 2 - k // 2) % (n // 2)) + ((j % 2) ^ (k % 2))
            left[j * rows : (j + 1) * rows, column] = att[k][source]
    middles[...] = dot(left[...], w_ref[:, :width])
    for j in range(n):
        middle = toks[j][...].astype(f32) + middles[j * rows : (j + 1) * rows]
        if j == 0:
            mid_ref[...] = middle
        inverse = lax.rsqrt(jnp.mean(middle * middle, axis=-1, keepdims=True) + epsilon)
        hid_ref[j] = (middle * inverse * gain_ref[0:1]).astype(bf16)
    for j in range(n):
        logits = dot(hid_ref[j], router)
        chosen = routes_ref[order[j]][:, 4 * HD :].astype(f32)
        chosen = jnp.concatenate([chosen, jnp.zeros((rows - TOP, rows), f32)], axis=0).T
        chosen = chosen.astype(jnp.int32)
        named = lane == chosen[:, 0:1]
        for k in range(1, TOP):
            named = jnp.logical_or(named, lane == chosen[:, k : k + 1])
        masked = jnp.where(named, logits, -1e30)
        top = jnp.max(masked, axis=-1, keepdims=True)
        e = jnp.where(named, jnp.exp(masked - top), 0.0)
        gates = e / jnp.sum(e, axis=-1, keepdims=True)
        if j == 0:
            gates_ref[...] = gates
        count = dot(before, named.astype(f32).astype(bf16))
        rank = jnp.where(named, count - 1.0, -1.0)
        rank_ref[j] = rank.T[:experts]
        gate_up_ref[j] = gates.T[:experts]


def middle_call(own, order, w, routes, att, toks, experts):
    n = len(att)
    rows, width = toks[0].shape
    return call(
        functools.partial(middle_kernel, n),
        [
            shape((n, rows, width), bf16),
            shape((rows, width), f32),
            shape((rows, 128), f32),
            shape((n, experts, rows), f32),
            shape((n, experts, rows), f32),
            shape((n * rows, width), bf16),
            shape((8, width), f32),
        ],
        2 * n * rows * width * (width + 128),
        2 * n * rows * width * 4,
        in_specs=[SMEM] * 2 + [VMEM] * (2 + 2 * n),
        out_specs=[VMEM] * 7,
        scratch_shapes=[pltpu.VMEM((n * rows, width), f32)],
    )(own, order, w, routes, *att, *toks)


def expert_kernel(
    first,
    hid_ref,
    cot_ref,
    swapped_ref,
    rank_ref,
    gate_ref,
    in_ref,
    out_ref,
    grad_ref,
    mix_keep,
    mix_swap,
    back_keep,
    back_swap,
    picks,
    xs,
    cots,
    gxs,
    mixes,
    backs,
    act_ref,
    gp_ref,
):
    e = pl.program_id(0)
    n, rows, width = hid_ref.shape
    here = xs.shape[0]
    slots = n * CAP
    experts = rank_ref.shape[1]

    @pl.when(e == 0)
    def _():
        slot = lax.broadcasted_iota(jnp.int32, (CAP, rows), 0).astype(f32)

        def gather(i, _):
            for b, source in ((2 * i, cot_ref), (2 * i + 1, swapped_ref)):
                own = pl.ds(pl.multiple_of(b * CAP, CAP), CAP)
                hots = [
                    (slot == rank_ref[b, pl.ds(first[0] + k, 1), :]).astype(f32)
                    for k in range(here)
                ]
                hot = jnp.concatenate(hots, axis=0)
                picks[b] = hot.T.astype(bf16)
                low = hot.astype(bf16)
                x = dot(low, hid_ref[b]).astype(bf16)
                g = dot(low, source[i])
                for k in range(here):
                    gate = jnp.sum(
                        hots[k] * gate_ref[b, pl.ds(first[0] + k, 1), :], axis=1, keepdims=True
                    )
                    part = slice(k * CAP, (k + 1) * CAP)
                    xs[k, own] = x[part]
                    cots[k, own] = g[part].astype(bf16)
                    gxs[k, own] = (gate * g[part]).astype(bf16)
                    mixes[k, own, :128] = jnp.broadcast_to(gate, (CAP, 128)).astype(f32)
            return 0

        lax.fori_loop(0, n // 2, gather, 0)

    w_in, w_out = in_ref[0], out_ref[0]
    half = slots // 2
    parts = [slice(0, half), slice(half, slots)]
    projected = [dot(xs[e, part], w_in) for part in parts]
    grad_active = [dot_t(gxs[e, part], w_out) for part in parts]
    lane = lax.broadcasted_iota(jnp.int32, (half, 128), 1)
    actives, gps = [], []
    for part, both, ga in zip(parts, projected, grad_active):
        gate_half = both[:, :F]
        up_half = both[:, F:]
        s = jax.nn.sigmoid(gate_half)
        silu = gate_half * s
        active = (silu * up_half).astype(bf16)
        gp = jnp.concatenate(
            [ga * up_half * s * (1.0 + gate_half * (1.0 - s)), ga * silu], axis=1
        ).astype(bf16)
        act_ref[part] = active
        gp_ref[part] = gp
        actives.append(active)
        gps.append(gp)
    for part, active, gp in zip(parts, actives, gps):
        produced = dot(active, w_out).astype(bf16).astype(f32)
        backs[e, part, :width] = dot_t(gp, w_in).astype(bf16)
        grad_gate = jnp.sum(cots[e, part].astype(f32) * produced, axis=-1, keepdims=True)
        high = grad_gate.astype(bf16).astype(f32)
        extra = jnp.where(lane == first[0] + e, high, 0.0) + jnp.where(
            lane == first[0] + e + experts, grad_gate - high, 0.0
        )
        backs[e, part, width:] = extra.astype(bf16)
        mixes[e, part] = mixes[e, part, :1] * produced
    n_out = grad_ref.shape[1]
    rows_in = width // n_out
    grad_ref[0, :, :rows_in] = t_dot(xs[e], gp_ref[...]).astype(bf16).reshape(n_out, rows_in, -1)
    grad_ref[0, :, rows_in:] = (
        t_dot(act_ref[...], gxs[e]).astype(bf16).reshape(n_out, F // n_out, -1)
    )

    @pl.when(e == here - 1)
    def _():

        def combine(i, _):
            for c, mix_ref, back_ref in ((0, mix_keep, back_keep), (1, mix_swap, back_swap)):
                b = 2 * i + c
                own = pl.ds(pl.multiple_of(b * CAP, CAP), CAP)
                pick = picks[b]
                mix = dot(
                    pick,
                    jnp.concatenate([mixes[k, own].astype(bf16) for k in range(here)], axis=0),
                )
                back = dot(pick, jnp.concatenate([backs[k, own] for k in range(here)], axis=0))
                mix_ref[i] = mix.astype(bf16)
                back_ref[i] = back.astype(bf16)
            return 0

        lax.fori_loop(0, n // 2, combine, 0)


def expert_call(first, hidden, cots, swapped, rank, gate, w_in, w_out, n_out):
    n, rows, width = hidden.shape
    here = w_in.shape[0]
    slots = n * CAP
    per = lambda *dims: pl.BlockSpec((1,) + dims, lambda e: (e, 0, 0))
    mix = shape((n // 2, rows, width), bf16)
    back = shape((n // 2, rows, width + 128), bf16)
    return call(
        expert_kernel,
        [
            shape((here, n_out, (width + F) // n_out, width), bf16),
            mix,
            mix,
            back,
            back,
        ],
        here * slots * width * F * 2 * 9,
        here * width * F * 6 + here * slots * width * 8,
        grid=(here,),
        in_specs=[SMEM] + [VMEM] * 5 + [per(width, 2 * F), per(F, width)],
        out_specs=[pl.BlockSpec((1, n_out, (width + F) // n_out, width), lambda e: (e, 0, 0, 0))]
        + [VMEM] * 4,
        scratch_shapes=[
            pltpu.VMEM((n, rows, here * CAP), bf16),
            pltpu.VMEM((here, slots, width), bf16),
            pltpu.VMEM((here, slots, width), bf16),
            pltpu.VMEM((here, slots, width), bf16),
            pltpu.VMEM((here, slots, width), f32),
            pltpu.VMEM((here, slots, width + 128), bf16),
            pltpu.VMEM((slots, F), bf16),
            pltpu.VMEM((slots, 2 * F), bf16),
        ],
    )(first, hidden, cots, swapped, rank, gate, w_in, w_out)


def norm_back_kernel(
    cot_ref, mid_ref, gates_ref, hid_ref, gain_ref, w_ref, *refs
):
    parts = refs[:4]
    gm_ref, send_ref, small_ref, gain_out = refs[4:]
    rows, width = mid_ref.shape
    got = parts[0][...].astype(f32)
    for part in parts[1:]:
        got = got + part[...].astype(f32)
    experts = 32
    extra = got[:, width:]
    grad_gates = extra + pltpu.roll(extra, 128 - experts, 1)
    gates = gates_ref[...]
    weighted = gates * grad_gates
    logits = (weighted - gates * jnp.sum(weighted, axis=-1, keepdims=True)).astype(bf16)
    grad = got[:, :width] + dot_t(logits, w_ref[:, width:])
    small_ref[...] = t_dot(hid_ref[0], logits)
    middle = mid_ref[...]
    inverse = lax.rsqrt(jnp.mean(middle * middle, axis=-1, keepdims=True) + epsilon)
    gain_out[...] = jnp.sum(grad * middle * inverse, axis=0, keepdims=True)
    scaled = grad * gain_ref[0:1]
    grad_middle = (
        cot_ref[...].astype(f32)
        + inverse * scaled
        - middle * (inverse * inverse * inverse) * jnp.mean(scaled * middle, axis=-1, keepdims=True)
    )
    gm_ref[...] = grad_middle
    branch = grad_middle.astype(bf16)
    attended = dot_t(branch, w_ref[:, :width]).astype(bf16)
    for e in range(send_ref.shape[0]):
        at = slice(e * 128, (e + 1) * 128)
        send_ref[e, :, :128] = attended[:, at]
        send_ref[e, :, 128:] = branch[:, at]


def norm_back_call(cot, middle, gates, hidden, gain, w, parts):
    rows, width = middle.shape
    n = hidden.shape[0]
    return call(
        norm_back_kernel,
        [
            shape((rows, width), f32),
            shape((n, rows, 256), bf16),
            shape((width, 128), f32),
            shape((1, width), f32),
        ],
        2 * rows * width * (width + 256),
        rows * width * 24 + 2 * width * width,
        grid=(1,),
        in_specs=[
            VMEM,
            VMEM,
            VMEM,
            pl.BlockSpec((1, rows, width), lambda i: (0, 0, 0)),
            VMEM,
            VMEM,
        ]
        + [VMEM] * 4,
        out_specs=[VMEM] * 4,
    )(cot, middle, gates, hidden, gain, w, *parts)


def key_grad_kernel(order, cos_ref, sin_ref, dq_ref, *refs):
    dkv = refs[:4]
    send_ref, up_ref = refs[4:]
    n, rows, _ = dq_ref.shape
    for j in range(n):
        kv = dkv[0][j].astype(f32)
        for other in dkv[1:]:
            kv = kv + other[j].astype(f32)
        up = kv.T
        up = jnp.concatenate([turn(up[:HD], cos_ref[j], -sin_ref[j]), up[HD:]], axis=0)
        up_ref[:, j * rows : (j + 1) * rows] = up.astype(bf16)
        send_ref[order[j], :, 2 * HD :] = up.T.astype(bf16)
        send_ref[j, :, : 2 * HD] = dq_ref[j]


def key_grad_call(order, cosine, sine, dq, dkv):
    n, rows, _ = dq.shape
    return whole(
        key_grad_kernel,
        [shape((n, rows, 4 * HD), bf16), shape((2 * HD, n * rows), bf16)],
        8,
        n * rows * 4 * HD * 10,
        n * rows * 4 * HD * 8,
        scalars=1,
    )(order, cosine, sine, dq, *dkv)


def key_weight_kernel(up_ref, hidden_ref, early_ref, out_ref):
    out_ref[:, : 4 * HD + 128] = early_ref[...]
    out_ref[:, 4 * HD + 128 :] = dot(up_ref[...], hidden_ref[...]).T.astype(bf16)


def key_weight_call(up, hidden, early):
    width = hidden.shape[1]
    return whole(
        key_weight_kernel,
        shape((width, 4 * HD + 256), bf16),
        3,
        2 * up.shape[0] * up.shape[1] * width,
        2 * width * (width + 1024),
    )(up, hidden, early)


def token_grad_kernel(got_ref, w_ref, tok_ref, mid_ref, out_ref):
    scaled = dot_t(got_ref[0], w_ref[0])
    for e in range(1, got_ref.shape[0]):
        scaled = scaled + dot_t(got_ref[e], w_ref[e])
    x = tok_ref[...].astype(f32)
    inverse = lax.rsqrt(jnp.mean(x * x, axis=-1, keepdims=True) + epsilon)
    out_ref[...] = (
        mid_ref[...]
        + inverse * scaled
        - x * (inverse * inverse * inverse) * jnp.mean(scaled * x, axis=-1, keepdims=True)
    )


def token_grad_call(got, w, tokens, grad_middle):
    rows, width = tokens.shape
    return whole(
        token_grad_kernel,
        shape((rows, width), f32),
        4,
        1000,
        1000,
    )(got, w, tokens, grad_middle)


def send_exp(x, dx, dc):
    n_x = lax.axis_size("exp") // 2
    pairs = [
        (2 * i + c, 2 * ((i + dx) % n_x) + (c ^ dc)) for i in range(n_x) for c in range(2)
    ]
    return lax.ppermute(x, "exp", pairs)


def send_ring(x, axis, d):
    n = lax.axis_size(axis)
    return lax.ppermute(x, axis, [(i, (i + d) % n) for i in range(n)])


def far_first(n):
    return sorted(range(1, n), key=lambda d: -min(d, n - d))


def gather_x(x):
    n_x = lax.axis_size("exp") // 2
    got = {dx: send_exp(x, n_x - dx, 0) for dx in far_first(n_x)}
    return [x] + [got[dx] for dx in range(1, n_x)]


def gather_cores(blocks):
    return [piece for block in blocks for piece in (block, send_exp(block, 0, 1))]


def gather_exp(x):
    return gather_cores(gather_x(x))


def chip_sums(keep, swap):
    got = send_exp(swap, 0, 1)
    return [
        (keep[dx].astype(f32) + got[dx].astype(f32)).astype(bf16) for dx in range(keep.shape[0])
    ]


def scatter_x(chip):
    got = {dx: send_exp(chip[dx], dx, 0) for dx in far_first(len(chip))}
    return [chip[0]] + [got[dx] for dx in range(1, len(chip))]


def gather_ring(x, axis):
    n = lax.axis_size(axis)
    got = {d: send_ring(x, axis, n - d) for d in far_first(n)}
    return [x] + [got[d] for d in range(1, n)]


def local(
    tokens,
    norm1_gain,
    w_query,
    w_keyval,
    w_output,
    norm2_gain,
    w_router,
    expert_in,
    expert_out,
    routes,
    cotangent,
):
    rows, width = tokens.shape
    experts = w_router.shape[1]
    n_rep, n_exp, n_seq = (lax.axis_size("rep"), lax.axis_size("exp"), lax.axis_size("seq"))
    shard = width // (n_rep * n_exp * n_seq)
    own_rep = lax.axis_index("rep")
    own_exp = lax.axis_index("exp")
    own_seq = lax.axis_index("seq")
    qcols = H // n_exp * HD
    here = expert_in.shape[0]
    n_x = n_exp // 2
    own = jnp.stack([own_exp // 2, lax.rem(own_exp, 2), own_seq]).astype(jnp.int32)
    relative = jnp.arange(n_exp, dtype=jnp.int32)
    order = 2 * lax.rem(own[0] + relative // 2, n_x) + lax.rem(own[1] + relative, 2)
    first = (own_exp * here).astype(jnp.int32).reshape(1)

    everyone = ("rep", "exp", "seq")
    n_all = n_rep * n_exp * n_seq

    columns, output_rows = pack_call(
        w_query,
        w_keyval,
        norm1_gain.reshape(1, shard),
        routes.T,
        w_output,
        w_router,
        norm2_gain.reshape(1, shard),
        n_exp,
    )
    columns = lax.all_to_all(columns, "exp", split_axis=0, concat_axis=0, tiled=True)
    columns, tokens_later = lax.optimization_barrier((columns, tokens))
    tok_blocks = gather_x(tokens_later)
    routes_g = columns
    columns = lax.all_to_all(
        jnp.broadcast_to(columns[None, :, :, : 4 * HD], (n_rep * n_seq, n_exp, shard, 4 * HD)),
        ("rep", "seq"),
        split_axis=0,
        concat_axis=0,
        tiled=True,
    )
    own_columns = (
        columns.reshape(n_rep, n_seq, n_exp, shard, 4 * HD)
        .transpose(0, 2, 1, 3, 4)
        .reshape(width, 4 * HD)
    )
    toks = gather_cores(tok_blocks)
    output_all = lax.all_gather(output_rows, everyone, axis=0, tiled=True)
    positions = (order[:, None] * n_seq + own_seq) * rows + jnp.arange(rows, dtype=jnp.int32)
    frequencies = 10000.0 ** (-(jnp.arange(HD // 2, dtype=f32) * 2.0 / HD))
    angles = positions.astype(f32)[:, None, :] * frequencies[None, :, None]
    cosine, sine = jnp.cos(angles), jnp.sin(angles)

    q, q_up, kv = qkv_call(toks, own_columns, cosine, sine)
    kv, cot = lax.optimization_barrier((kv, cotangent))
    kvs, cots = lax.optimization_barrier((gather_ring(kv, "seq"), gather_x(cot)))
    attended, att_up, log_total = attend_call(own, q_up, kvs)
    attended, cots = lax.optimization_barrier((attended, jnp.stack(cots)))
    cots_swapped = send_exp(cots, 0, 1)
    attended, own_columns = lax.optimization_barrier((gather_exp(attended), own_columns))
    qkv_all = lax.all_gather(own_columns, "exp", axis=0)
    hidden2, middle, gates, rank, gate_up, left, gains = middle_call(
        own, order, output_all, routes_g, attended, toks, experts
    )
    expert_grads, mix_keep, mix_swap, back_keep, back_swap = expert_call(
        first,
        hidden2,
        cots,
        cots_swapped,
        rank,
        gate_up,
        expert_in,
        expert_out,
        n_rep * n_seq,
    )

    expert_grads = lax.psum_scatter(
        expert_grads.reshape(here, -1, width), ("rep", "seq"), scatter_dimension=1, tiled=True
    ).astype(f32)
    parts = scatter_x(chip_sums(back_keep, back_swap))
    rows_in = width // (n_rep * n_seq)
    grad_expert_in = expert_grads[:, :rows_in]
    grad_expert_out = expert_grads[:, rows_in:]
    grad_middle, send, grad_router, grad_gain_two = norm_back_call(
        cotangent, middle, gates, hidden2, gains, output_all, parts
    )
    send, mix_keep, mix_swap = lax.optimization_barrier((send, mix_keep, mix_swap))
    mix = chip_sums(mix_keep, mix_swap)
    got = lax.all_to_all(send, "exp", split_axis=0, concat_axis=0, tiled=True)
    mix = scatter_x(mix)
    dq, *dkv = attend_back_call(own, q, q_up, att_up, log_total, got, cosine, sine, kvs)
    dkv, mix = lax.optimization_barrier((dkv, mix))
    output = (middle + sum(piece.astype(f32) for piece in mix)).astype(bf16)
    sent = {d: send_ring(dkv[d], "seq", d) for d in far_first(n_seq)}
    dkv = [dkv[0]] + [sent[d] for d in range(1, n_seq)]
    dkv[1], dq = lax.optimization_barrier((dkv[1], dq))
    early, hidden1 = early_call(order, left, dq, got, grad_router, grad_gain_two, toks)
    dq, early = lax.optimization_barrier((dq, early))
    send, dkv_up = key_grad_call(order, cosine, sine, dq, dkv)
    got = lax.all_to_all(send, "exp", split_axis=0, concat_axis=0, tiled=True)
    dense = key_weight_call(dkv_up, hidden1, early)
    got, _ = lax.optimization_barrier((got, dense))
    dense = lax.all_to_all(
        dense.reshape(n_all, shard, -1), everyone, split_axis=0, concat_axis=0, tiled=True
    )
    grad_tokens = token_grad_call(got, qkv_all, tokens, grad_middle)
    dense, grad_tokens, grad_expert_in, grad_expert_out = lax.optimization_barrier(
        (dense, grad_tokens, grad_expert_in, grad_expert_out)
    )
    grad_query, grad_keyval, grad_output, grad_router, grad_gain_one, grad_gain_two = unpack_call(
        dense, w_query, w_keyval, norm1_gain.reshape(1, shard), experts, n_exp, n_seq
    )
    return (
        output,
        grad_tokens,
        grad_gain_one.reshape(shard),
        grad_query,
        grad_keyval,
        grad_output,
        grad_gain_two.reshape(shard),
        grad_router,
        grad_expert_in,
        grad_expert_out,
    )


def solution(mesh):
    placed = (
        P(("rep", "exp", "seq"), None),
        P(("rep", "exp", "seq")),
        P(("rep", "exp", "seq"), None),
        P(("rep", "exp", "seq"), None),
        P(("rep", "exp", "seq"), None),
        P(("rep", "exp", "seq")),
        P(("rep", "exp", "seq"), None),
        P("exp", None, None),
        P("exp", None, None),
        P(("rep", "exp", "seq"), None),
        P(("rep", "exp", "seq"), None),
    )
    return jax.shard_map(
        local,
        mesh=mesh,
        in_specs=placed,
        out_specs=(
            P(("rep", "exp", "seq"), None),
            P(("rep", "exp", "seq"), None),
            P(("rep", "exp", "seq")),
            P(("rep", "exp", "seq"), None),
            P(("rep", "exp", "seq"), None),
            P(("rep", "exp", "seq"), None),
            P(("rep", "exp", "seq")),
            P(("rep", "exp", "seq"), None),
            P("exp", ("rep", "seq"), None),
            P("exp", ("rep", "seq"), None),
        ),
        check_vma=False,
    )
```
